256 devices in a mesh: mem: 8 (over x, y_lo), tile: 32 (over z, y_hi, core).
Axes of the slice: x: 4, y: 4 (y_hi: 2, y_lo: 2; y = y_hi * 2 + y_lo), z: 8, core: 2. Of those that a mesh axis runs over, the one named last changes fastest.
Arguments:
- ensemble: bfloat16 [64, 72, 512, 128], P('mem', None, 'tile'), may hold values from -6 to 6
- weights: bfloat16 [1024, 64, 64], P('tile'), may hold values from -0.75 to 0.75
- patch_index: int32 [512, 128], P('tile'), may hold values from 0 to 31
- courant: float32 [2, 72, 512, 128], P(None, None, 'tile'), may hold values from -0.95 to 0.95
- vert_inverse: bfloat16 [512, 72, 72], P('tile'), may hold values from -0.23570226 to 1.2357023
Outputs:
- forecast: bfloat16 [64, 72, 512, 128], P('mem', None, 'tile')
The draws below stay inside these ranges and needn't reach their ends.
All inputs are finite; a program needn't handle non-finite values.
Results may differ from the reference program's by a relative error of at most 0.0078.
Values may be sent and summed in bfloat16 or wider, within the bound.
No kernel may reach another device: no remote copies, remote signals or barrier semaphores. Data moves between devices by JAX's collectives and lax.ppermute only.
A program may use at most 192 MiB of HBM per device.

```python
import math
import jax
import jax.numpy as jnp
from jax import lax

E = 64
L = 72
LON_DEV = 16
LAT = 128
PATCH_DEV = 32
STEPS = 6
NLON = 512
WEIGHT_PATCHES = 1024


def draw_vert_inverse(key, part):
    key = jax.random.fold_in(key, 11)
    identity = jnp.eye(L, dtype=jnp.float32)
    normals = jnp.clip(jax.random.normal(key, (NLON, L, L), jnp.float32), -4.0, 4.0)
    return (identity[None, :, :] + 0.5 * normals / math.sqrt(L)).astype(jnp.bfloat16)


def with_ends(array, key, low, top_value):
    place = [jax.random.randint(jax.random.fold_in(key, axis), (), 0, length) for axis, length in enumerate(array.shape)]
    widest = array.shape.index(max(array.shape))
    beside = place[:widest] + [(place[widest] + 1) % array.shape[widest]] + place[widest + 1:]
    return array.at[tuple(place)].set(low).at[tuple(beside)].set(top_value)


def shard_levels(stream_key, shape, shards, low, top_value):
    gain, own = 1.0, jax.random.fold_in(stream_key, 6)
    for axis_at, shards_of in shards:
        draws = jnp.exp(jax.random.uniform(jax.random.fold_in(own, axis_at), (shards_of,), jnp.float32, low / len(shards), top_value / len(shards)))
        gain = gain * jnp.repeat(draws, shape[axis_at] // shards_of).reshape([-1 if axis == axis_at else 1 for axis in range(len(shape))])
    return gain


def scatter_about(key, extent, scale, bound, shards=(), kind=jnp.bfloat16):
    loudness = shard_levels(key, extent, shards, -0.22, 0.18) if shards else 1.0
    values = jax.random.normal(key, extent, jnp.float32) * scale * loudness
    return jnp.minimum(jnp.maximum(values, -bound), bound).astype(kind)


def setup_inputs(seed: int = 0) -> dict:
    streams_of = jax.random.split(jax.random.key(seed), 6)
    ensemble = scatter_about(streams_of[0], (E, L, NLON, LAT), 1.0, 6.0, ((0, 8), (2, 32)))
    weights = scatter_about(streams_of[1], (WEIGHT_PATCHES, E, E), E ** -0.5, 0.75, ((0, 32),))
    patch_index = with_ends(jax.random.randint(streams_of[2], (NLON, LAT), 0, PATCH_DEV), jax.random.fold_in(streams_of[2], 1), 0, PATCH_DEV - 1).astype(jnp.int32)
    courant = jnp.clip(jax.random.uniform(streams_of[3], (2, L, NLON, LAT), jnp.float32, -0.95, 0.95) * shard_levels(streams_of[3], (2, L, NLON, LAT), ((2, 32),), -0.4, 0.0), -0.95, 0.95)
    vert_inverse = draw_vert_inverse(jax.random.fold_in(streams_of[5], 71), 0)
    return {"ensemble": ensemble, "weights": weights, "patch_index": patch_index, "courant": courant, "vert_inverse": vert_inverse}


def upstream(padded, tracer_numbers, dimension):
    length = padded.shape[dimension] - 4

    def shifted_field(offset):
        return lax.slice_in_dim(padded, 2 + offset, 2 + offset + length, axis=dimension)

    location = -jnp.abs(tracer_numbers)
    weight_far = -(location + 1.0) * location * (location - 1.0) / 6.0
    weight_near = (location + 2.0) * location * (location - 1.0) / 2.0
    weight_mid = -(location + 2.0) * (location + 1.0) * (location - 1.0) / 2.0
    weight_ahead = (location + 2.0) * (location + 1.0) * location / 6.0
    forward = tracer_numbers >= 0.0
    return (weight_far * jnp.where(forward, shifted_field(-2), shifted_field(2))
            + weight_near * jnp.where(forward, shifted_field(-1), shifted_field(1))
            + weight_mid * shifted_field(0)
            + weight_ahead * jnp.where(forward, shifted_field(1), shifted_field(-1)))


def reference(ensemble, weights, patch_index, courant, vert_inverse):
    tiles = jnp.arange(NLON, dtype=jnp.int32) // LON_DEV
    global_patch = (tiles[:, None] * PATCH_DEV + patch_index).astype(jnp.int32)

    def analyse(index):
        matrices = jnp.take(weights, global_patch[index], axis=0).astype(jnp.float32)
        columns = lax.dynamic_index_in_dim(ensemble, index, 2, keepdims=False).astype(jnp.float32)
        return jnp.einsum("pjo,jlp->olp", matrices, columns).astype(jnp.bfloat16)

    analysed_state = lax.map(analyse, jnp.arange(NLON, dtype=jnp.int32))
    analysed_state = lax.optimization_barrier(jnp.transpose(analysed_state, (1, 2, 0, 3)))
    inverse_wide = vert_inverse.astype(jnp.float32)

    def prior_member_field(member_state):
        tracer = member_state
        for section in range(STEPS):
            extended = jnp.pad(tracer.astype(jnp.float32), ((0, 0), (2, 2), (0, 0)), mode="wrap")
            along_lon = upstream(extended, courant[0], 1)
            padded = jnp.pad(along_lon, ((0, 0), (0, 0), (2, 2)))
            across = upstream(padded, courant[1], 2).astype(jnp.bfloat16)
            across = lax.optimization_barrier(across).astype(jnp.float32)
            tracer = jnp.einsum("ikl,lij->kij", inverse_wide, across).astype(jnp.bfloat16)
            tracer = lax.optimization_barrier(tracer)
        return tracer

    return lax.map(prior_member_field, analysed_state)
```

```python
import functools

import jax
import jax.numpy as jnp
from jax import lax
from jax.experimental import pallas as pl
from jax.experimental.pallas import tpu as pltpu
from jax.sharding import PartitionSpec as P

ROUNDS = (3, 3)
GROUPS = 2
LEVELS = 72
PAIR = 2 * LEVELS
TILE_ROWS = 16
WEIGHT_ROWS = LEVELS + 8
LANES = 128


def stencil_weights(numbers):
    location = -jnp.abs(numbers)
    far = -(location + 1.0) * location * (location - 1.0) / 6.0
    near = (location + 2.0) * location * (location - 1.0) / 2.0
    mid = -(location + 2.0) * (location + 1.0) * (location - 1.0) / 2.0
    ahead = (location + 2.0) * (location + 1.0) * location / 6.0
    forward = numbers >= 0.0
    zero = jnp.zeros_like(far)
    return [
        jnp.where(forward, far, zero),
        jnp.where(forward, near, ahead),
        mid,
        jnp.where(forward, ahead, near),
        jnp.where(forward, zero, far),
    ]


def column_weights(numbers):
    numbers = jnp.transpose(numbers, (2, 0, 1, 3))
    lon = stencil_weights(numbers[:, 0])
    lat = stencil_weights(numbers[:, 1])
    row = lax.broadcasted_iota(jnp.int32, lat[0].shape, 2)
    last = LANES - 1
    inside = [row >= 2, row >= 1, row >= 0, row <= last - 1, row <= last - 2]
    lat = [jnp.where(keep, weight, 0.0) for keep, weight in zip(inside, lat)]
    both = jnp.stack(lon + lat, axis=1)
    return jnp.concatenate([both, both[:, :, :8]], axis=2)


def weighted(values, weights):
    total = values[0] * weights[0]
    for value, weight in zip(values[1:], weights[1:]):
        total = total + value * weight
    return total


def advect_kernel(steps, rows, before, owned, after, weights, inverse, out, field, other, across_0, across_1,
                  weight, operator, field_sem, weight_sem, operator_sem):
    halo = 2 * steps
    length = owned.shape[0]
    computed = weight.shape[0]
    first = (computed - (length + 4 * (steps - 1))) // 2
    parts = ((before, 0, halo), (owned, halo, length), (after, halo + length, halo))
    loads = [pltpu.make_async_copy(ref, field.at[pl.ds(at, count)], field_sem.at[index])
             for index, (ref, at, count) in enumerate(parts)]
    loads.append(pltpu.make_async_copy(inverse, operator, operator_sem))
    for load in loads:
        load.start()

    def weight_load(column):
        return pltpu.make_async_copy(weights.at[column], weight.at[column], weight_sem.at[column])

    def start_load(column, carry):
        weight_load(column).start()
        return carry

    lax.fori_loop(first, computed - first, start_load, 0)
    for load in loads:
        load.wait()

    pairs = rows // PAIR

    def stencils(source, column, w_column, across):
        for tile in range(PAIR // TILE_ROWS):
            level = (tile * TILE_ROWS) % LEVELS
            w = [weight[w_column, k, pl.ds(level, TILE_ROWS), :] for k in range(10)]
            for pair in range(pairs):
                at = pl.ds(pair * PAIR + tile * TILE_ROWS, TILE_ROWS)
                values = [source[column + k, at, :].astype(jnp.float32) for k in range(5)]
                along = weighted(values, w[:5])
                shifted = [pltpu.roll(along, 2, 1), pltpu.roll(along, 1, 1), along,
                           pltpu.roll(along, LANES - 1, 1), pltpu.roll(along, LANES - 2, 1)]
                across[at, :] = weighted(shifted, w[5:]).astype(jnp.bfloat16)

    def vertical(across, target, column, w_column):
        side = jnp.concatenate([across[pl.ds(pair * PAIR, PAIR), :] for pair in range(pairs)], axis=1)
        mixed = jnp.dot(operator[w_column], side, preferred_element_type=jnp.float32).astype(jnp.bfloat16)
        for pair in range(pairs):
            target[column, pl.ds(pair * PAIR, PAIR), :] = mixed[:, pair * LANES:(pair + 1) * LANES]

    buffers = (field, other)
    for step in range(steps):
        source = buffers[step % 2]
        target = out if step == steps - 1 else buffers[(step + 1) % 2]
        columns = length + 4 * (steps - 1 - step)
        shift = first + 2 * step

        def arrive(column):
            if step == 0:
                weight_load(column).wait()

        arrive(shift)
        stencils(source, 0, shift, across_0)

        def pair_of_columns(index, carry):
            even = 2 * index
            arrive(shift + even + 1)
            vertical(across_0, target, even, shift + even)
            stencils(source, even + 1, shift + even + 1, across_1)
            arrive(shift + even + 2)
            vertical(across_1, target, even + 1, shift + even + 1)
            stencils(source, even + 2, shift + even + 2, across_0)
            return carry

        lax.fori_loop(0, columns // 2 - 1, pair_of_columns, 0)
        even = columns - 2
        arrive(shift + even + 1)
        vertical(across_0, target, even, shift + even)
        stencils(source, even + 1, shift + even + 1, across_1)
        vertical(across_1, target, even + 1, shift + even + 1)


def advect(steps, before, owned, after, weights, inverse):
    length, rows, lanes = owned.shape
    computed = weights.shape[0]
    anywhere = pl.BlockSpec(memory_space=pl.ANY)
    work = (length + 2 * steps) * steps * rows * lanes
    return pl.pallas_call(
        functools.partial(advect_kernel, steps, rows),
        out_shape=jax.ShapeDtypeStruct(owned.shape, owned.dtype),
        in_specs=[anywhere] * 5,
        out_specs=pl.BlockSpec(memory_space=pltpu.VMEM),
        scratch_shapes=[
            pltpu.VMEM((length + 4 * steps, rows, lanes), jnp.bfloat16),
            pltpu.VMEM((length + 4 * steps, rows, lanes), jnp.bfloat16),
            pltpu.VMEM((rows, lanes), jnp.bfloat16),
            pltpu.VMEM((rows, lanes), jnp.bfloat16),
            pltpu.VMEM(weights.shape, jnp.float32),
            pltpu.VMEM(inverse.shape, jnp.bfloat16),
            pltpu.SemaphoreType.DMA((3,)),
            pltpu.SemaphoreType.DMA((computed,)),
            pltpu.SemaphoreType.DMA,
        ],
        compiler_params=pltpu.CompilerParams(vmem_limit_bytes=30 * 1024 * 1024),
        cost_estimate=pl.CostEstimate(flops=work * (2 * LEVELS + 20), bytes_accessed=weights.size * 4, transcendentals=0),
    )(before, owned, after, weights, inverse)


def from_sides(array, width, dim):
    peers, length = lax.axis_size("tile"), array.shape[dim]
    up = [(i, (i + 1) % peers) for i in range(peers)]
    down = [(j, i) for i, j in up]
    before = lax.ppermute(lax.slice_in_dim(array, length - width, length, axis=dim), "tile", up)
    after = lax.ppermute(lax.slice_in_dim(array, 0, width, axis=dim), "tile", down)
    return before, after


def extended(array, width, dim):
    before, after = from_sides(array, width, dim)
    return jnp.concatenate([before, array, after], axis=dim)


def shards(ensemble, weights, patch_index, courant, vert_inverse):
    peers = lax.axis_size("mem")
    members, levels, length, lanes = ensemble.shape
    share = length // peers
    margin = 2 * (max(ROUNDS) - 1)

    to_send = jnp.transpose(ensemble, (2, 0, 1, 3)).reshape(peers, share, members, levels, lanes)
    arrived = lax.all_to_all(to_send, "mem", split_axis=0, concat_axis=0, tiled=True)

    patches = lax.dynamic_slice_in_dim(patch_index, lax.axis_index("mem") * share, share, 0)
    chosen = jnp.take(weights, patches, axis=0)
    numbers = column_weights(extended(courant, margin, 2))
    inverse = extended(vert_inverse, margin, 0)
    empty = jnp.zeros_like(inverse)
    inverse = jnp.concatenate([jnp.concatenate([inverse, empty], 2), jnp.concatenate([empty, inverse], 2)], 1)

    blended = jnp.einsum("ijco,iclj->iolj", chosen,
                         jnp.transpose(arrived, (1, 0, 2, 3, 4)).reshape(share, -1, levels, lanes),
                         preferred_element_type=jnp.float32).astype(jnp.bfloat16)
    blended = jnp.transpose(blended.reshape(share, peers, members, levels, lanes), (1, 0, 2, 3, 4))
    analysed = lax.all_to_all(blended, "mem", split_axis=0, concat_axis=0, tiled=True)
    fields = analysed.reshape(length, GROUPS, -1, lanes)
    fields = [fields[:, group] for group in range(GROUPS)]
    for steps in ROUNDS:
        sides = [from_sides(field, 2 * steps, 0) for field in fields]
        fields = [advect(steps, before, field, after, numbers, inverse)
                  for field, (before, after) in zip(fields, sides)]
    forecast = jnp.stack(fields, axis=1).reshape(length, members, levels, lanes)
    return jnp.transpose(forecast, (1, 2, 0, 3))


def solution(mesh):
    return jax.shard_map(
        shards,
        mesh=mesh,
        in_specs=(
            P("mem", None, "tile", None),
            P("tile", None, None),
            P("tile", None),
            P(None, None, "tile", None),
            P("tile", None, None),
        ),
        out_specs=P("mem", None, "tile", None),
        check_vma=False,
    )
```

```python
import functools

import jax
import jax.numpy as jnp
from jax import lax
from jax.experimental import pallas as pl
from jax.experimental.pallas import tpu as pltpu
from jax.sharding import PartitionSpec as P

HALF = 3
GROUPS = 2
LEVELS = 72
PAIR = 2 * LEVELS
TILE_ROWS = 16
LANES = 128


def stencil_weights(numbers):
    location = -jnp.abs(numbers)
    below, above, further = location - 1.0, location + 1.0, location + 2.0
    inner, outer = location * below, further * above
    far = above * inner * (-1.0 / 6.0)
    near = further * inner * 0.5
    mid = outer * below * -0.5
    ahead = outer * location * (1.0 / 6.0)
    forward = numbers >= 0.0
    return [
        jnp.where(forward, far, 0.0),
        jnp.where(forward, near, ahead),
        mid,
        jnp.where(forward, ahead, near),
        jnp.where(forward, 0.0, far),
    ]


def weighted(values, weights):
    total = values[0] * weights[0]
    for value, weight in zip(values[1:], weights[1:]):
        total = total + value * weight
    return total


def advect_kernel(steps, first, low, high, numbers, inverse, out, staged, field, other, across_0, across_1,
                  number, weight, operator, field_sem, number_sem, operator_sem):
    length, rows, _ = out.shape
    computed = length + 4 * (steps - 1)
    pairs = rows // PAIR
    loads = [
        pltpu.make_async_copy(low, staged.at[pl.ds(0, low.shape[0])], field_sem.at[0]),
        pltpu.make_async_copy(high, staged.at[pl.ds(low.shape[0], high.shape[0])], field_sem.at[1]),
        pltpu.make_async_copy(numbers.at[pl.ds(first, computed)], number, number_sem),
        pltpu.make_async_copy(inverse.at[pl.ds(first, computed)], operator, operator_sem),
    ]
    for load in loads:
        load.start()
    for load in loads:
        load.wait()

    lane = lax.broadcasted_iota(jnp.int32, (8, LANES), 1)
    last = LANES - 1
    inside = [lane >= 2, lane >= 1, None, lane <= last - 1, lane <= last - 2]

    def prepare(column):
        for level in range(0, LEVELS, 8):
            at = pl.ds(level, 8)
            lon = stencil_weights(number[column, 0, at, :])
            lat = stencil_weights(number[column, 1, at, :])
            lat = [w if keep is None else jnp.where(keep, w, 0.0) for keep, w in zip(inside, lat)]
            for k, w in enumerate(lon + lat):
                weight[column, k, at, :] = w
                if level == 0:
                    weight[column, k, pl.ds(LEVELS, 8), :] = w

    def widen(column):
        field[column] = staged[column].astype(jnp.float32)

    def stencils(source, column, w_column, across):
        def lat_part(at, along, w):
            near = along.astype(jnp.bfloat16)
            shifted = [pltpu.roll(near, turn, 1).astype(jnp.float32) if turn else along
                       for turn in (2, 1, 0, LANES - 1, LANES - 2)]
            across[at, :] = weighted(shifted, w).astype(jnp.bfloat16)

        for tile in range(PAIR // TILE_ROWS):
            level = (tile * TILE_ROWS) % LEVELS
            w = [weight[w_column, k, pl.ds(level, TILE_ROWS), :] for k in range(10)]
            for pair in range(pairs):
                at = pl.ds(pair * PAIR + tile * TILE_ROWS, TILE_ROWS)
                lat_part(at, weighted([source[column + k, at, :] for k in range(5)], w[:5]), w[5:])

    def vertical(across, target, column, w_column):
        side = jnp.concatenate([across[pl.ds(pair * PAIR, PAIR), :] for pair in range(pairs)], axis=1)
        mixed = jnp.dot(operator[w_column], side, preferred_element_type=jnp.float32).astype(jnp.bfloat16)
        for pair in range(pairs):
            target[column, pl.ds(pair * PAIR, PAIR), :] = mixed[:, pair * LANES:(pair + 1) * LANES].astype(target.dtype)

    buffers = (field, other)
    for step in range(steps):
        source = buffers[step % 2]
        target = out if step == steps - 1 else buffers[(step + 1) % 2]
        columns = length + 4 * (steps - 1 - step)
        shift = 2 * step

        def ready(column):
            if step == 0:
                widen(column + 4)
                prepare(column)

        if step == 0:
            for column in range(4):
                widen(column)
        ready(0)
        ready(1)
        stencils(source, 0, shift, across_0)
        stencils(source, 1, shift + 1, across_1)

        def two_columns(index, carry):
            even = 2 * index
            vertical(across_0, target, even - 2, shift + even - 2)
            vertical(across_1, target, even - 1, shift + even - 1)
            ready(even)
            ready(even + 1)
            stencils(source, even, shift + even, across_0)
            stencils(source, even + 1, shift + even + 1, across_1)
            return carry

        lax.fori_loop(1, columns // 2, two_columns, 0)
        vertical(across_0, target, columns - 2, shift + columns - 2)
        vertical(across_1, target, columns - 1, shift + columns - 1)


def advect(steps, first, low, high, numbers, inverse):
    rows, lanes = low.shape[1:]
    wide = low.shape[0] + high.shape[0]
    length, computed = wide - 4 * steps, wide - 4
    anywhere = pl.BlockSpec(memory_space=pl.ANY)
    work = (length + 2 * steps) * steps * rows * lanes
    return pl.pallas_call(
        functools.partial(advect_kernel, steps, first),
        out_shape=jax.ShapeDtypeStruct((length, rows, lanes), low.dtype),
        in_specs=[anywhere] * 4,
        out_specs=pl.BlockSpec(memory_space=pltpu.VMEM),
        scratch_shapes=[
            pltpu.VMEM((wide, rows, lanes), jnp.bfloat16),
            pltpu.VMEM((wide, rows, lanes), jnp.float32),
            pltpu.VMEM((wide, rows, lanes), jnp.float32),
            pltpu.VMEM((rows, lanes), jnp.bfloat16),
            pltpu.VMEM((rows, lanes), jnp.bfloat16),
            pltpu.VMEM((computed,) + numbers.shape[1:], jnp.float32),
            pltpu.VMEM((computed, 10, LEVELS + 8, lanes), jnp.float32),
            pltpu.VMEM((computed,) + inverse.shape[1:], jnp.bfloat16),
            pltpu.SemaphoreType.DMA((2,)),
            pltpu.SemaphoreType.DMA,
            pltpu.SemaphoreType.DMA,
        ],
        compiler_params=pltpu.CompilerParams(vmem_limit_bytes=36 * 1024 * 1024),
        cost_estimate=pl.CostEstimate(flops=work * (2 * LEVELS + 20), bytes_accessed=numbers.size * 4, transcendentals=0),
    )(low, high, numbers, inverse)


def from_below(array, width):
    peers = lax.axis_size("tile")
    return lax.ppermute(array[array.shape[0] - width:], "tile", [(i, (i + 1) % peers) for i in range(peers)])


def from_above(array, width):
    peers = lax.axis_size("tile")
    return lax.ppermute(array[:width], "tile", [((i + 1) % peers, i) for i in range(peers)])


def shards(ensemble, weights, patch_index, courant, vert_inverse):
    peers = lax.axis_size("mem")
    members, levels, length, lanes = ensemble.shape
    share = length // peers
    halo, shift = 4 * HALF, 2 * HALF
    below, above = shift - 2, halo - 2

    to_send = jnp.transpose(ensemble.reshape(members, levels, peers, share, lanes), (3, 2, 0, 1, 4))
    patches = lax.dynamic_slice_in_dim(patch_index, lax.axis_index("mem") * share, share, 0)
    chosen = jnp.take(weights, patches, axis=0)

    arrived = [lax.all_to_all(to_send[part], "mem", split_axis=0, concat_axis=0, tiled=True) for part in range(share)]
    tied, _ = lax.optimization_barrier(((courant, vert_inverse), to_send))
    numbers, inverse = jnp.transpose(tied[0], (2, 0, 1, 3)), tied[1]
    numbers = jnp.concatenate([from_below(numbers, below), numbers, from_above(numbers, above)])
    inverse = jnp.concatenate([from_below(inverse, below), inverse, from_above(inverse, above)])
    empty = jnp.zeros_like(inverse)
    inverse = jnp.concatenate([jnp.concatenate([inverse, empty], 2), jnp.concatenate([empty, inverse], 2)], 1)

    returned = []
    for part in range(share):
        blended = jnp.einsum("jco,clj->olj", chosen[part], arrived[part].reshape(-1, levels, lanes),
                             preferred_element_type=jnp.float32).astype(jnp.bfloat16)
        blended = blended.reshape(arrived[part].shape)
        returned.append(lax.all_to_all(blended, "mem", split_axis=0, concat_axis=0, tiled=True))
    analysed = jnp.stack(returned, axis=1).reshape(length, GROUPS, -1, lanes)
    fields = [analysed[:, group] for group in range(GROUPS)]
    fields = [advect(HALF, below + 2, field, from_above(field, halo), numbers, inverse) for field in fields]
    fields = [advect(HALF, 0, from_below(field, halo), field, numbers, inverse) for field in fields]
    forecast = jnp.stack(fields, axis=1).reshape(length, members, levels, lanes)
    return jnp.transpose(forecast, (1, 2, 0, 3))


def solution(mesh):
    return jax.shard_map(
        shards,
        mesh=mesh,
        in_specs=(
            P("mem", None, "tile", None),
            P("tile", None, None),
            P("tile", None),
            P(None, None, "tile", None),
            P("tile", None, None),
        ),
        out_specs=P("mem", None, "tile", None),
        check_vma=False,
    )
```

```python
import functools
import math

import jax
import jax.numpy as jnp
from jax import lax
from jax.experimental import pallas as pl
from jax.experimental.pallas import tpu as pltpu
from jax.sharding import PartitionSpec as P

HALF = 3
GROUPS = 2
LEVELS = 72
PAIR = 2 * LEVELS
TILE_ROWS = 16
LANES = 128


def stencil_weights(numbers):
    location = -jnp.abs(numbers)
    below, above, further = location - 1.0, location + 1.0, location + 2.0
    inner, outer = location * below, further * above
    far = above * inner * (-1.0 / 6.0)
    near = further * inner * 0.5
    mid = outer * below * -0.5
    ahead = outer * location * (1.0 / 6.0)
    forward = numbers >= 0.0
    return [
        jnp.where(forward, far, 0.0),
        jnp.where(forward, near, ahead),
        mid,
        jnp.where(forward, ahead, near),
        jnp.where(forward, 0.0, far),
    ]


def weighted(values, weights):
    total = values[0] * weights[0]
    for value, weight in zip(values[1:], weights[1:]):
        total = total + value * weight
    return total


def advect_kernel(steps, places, *refs):
    parts, (numbers, inverse, out), scratch = refs[:len(places)], refs[len(places):len(places) + 3], refs[len(places) + 3:]
    staged, field, other, across_0, across_1, number, weight, operator, field_sem, number_sem, operator_sem = scratch
    length, rows, _ = out.shape
    computed = length + 4 * (steps - 1)
    pairs = rows // PAIR
    loads = [
        pltpu.make_async_copy(numbers, number, number_sem),
        pltpu.make_async_copy(inverse, operator, operator_sem),
    ]
    for index, (ref, place) in enumerate(zip(parts, places)):
        group, start, offset = place
        source = ref if group is None else ref.at[:, group]
        target = staged.at[pl.ds(start, ref.shape[0]), offset] if offset is not None else staged.at[pl.ds(start, ref.shape[0])]
        loads.append(pltpu.make_async_copy(source, target, field_sem.at[index]))
    for load in loads:
        load.start()
    for load in loads:
        load.wait()

    lane = lax.broadcasted_iota(jnp.int32, (8, LANES), 1)
    last = LANES - 1
    inside = [lane >= 2, lane >= 1, None, lane <= last - 1, lane <= last - 2]

    def prepare(column):
        for level in range(0, LEVELS, 8):
            at = pl.ds(level, 8)
            lon = stencil_weights(number[column, 0, at, :])
            lat = stencil_weights(number[column, 1, at, :])
            lat = [w if keep is None else jnp.where(keep, w, 0.0) for keep, w in zip(inside, lat)]
            for k, w in enumerate(lon + lat):
                weight[column, k, at, :] = w
                if level == 0:
                    weight[column, k, pl.ds(LEVELS, 8), :] = w

    def widen(column):
        if len(staged.shape) == 4:
            held = staged[column // 2, column % 2]
        else:
            held = staged[column]
        field[column] = held.astype(jnp.float32)

    def stencils(source, column, w_column, across):
        def lat_part(at, along, w):
            near = along.astype(jnp.bfloat16)
            shifted = [pltpu.roll(near, turn, 1).astype(jnp.float32) if turn else along
                       for turn in (2, 1, 0, LANES - 1, LANES - 2)]
            across[at, :] = weighted(shifted, w).astype(jnp.bfloat16)

        for tile in range(PAIR // TILE_ROWS):
            level = (tile * TILE_ROWS) % LEVELS
            w = [weight[w_column, k, pl.ds(level, TILE_ROWS), :] for k in range(10)]
            for pair in range(pairs):
                at = pl.ds(pair * PAIR + tile * TILE_ROWS, TILE_ROWS)
                lat_part(at, weighted([source[column + k, at, :] for k in range(5)], w[:5]), w[5:])

    def vertical(across, target, column, w_column):
        side = jnp.concatenate([across[pl.ds(pair * PAIR, PAIR), :] for pair in range(pairs)], axis=1)
        mixed = jnp.dot(operator[w_column], side, preferred_element_type=jnp.float32).astype(jnp.bfloat16)
        for pair in range(pairs):
            target[column, pl.ds(pair * PAIR, PAIR), :] = mixed[:, pair * LANES:(pair + 1) * LANES].astype(target.dtype)

    buffers = (field, other)
    for step in range(steps):
        source = buffers[step % 2]
        target = out if step == steps - 1 else buffers[(step + 1) % 2]
        columns = length + 4 * (steps - 1 - step)
        shift = 2 * step

        def ready(column):
            if step == 0:
                widen(column + 4)
                prepare(column)

        if step == 0:
            for column in range(4):
                widen(column)
        ready(0)
        ready(1)
        stencils(source, 0, shift, across_0)
        stencils(source, 1, shift + 1, across_1)

        def two_columns(index, carry):
            even = 2 * index
            vertical(across_0, target, even - 2, shift + even - 2)
            vertical(across_1, target, even - 1, shift + even - 1)
            ready(even)
            ready(even + 1)
            stencils(source, even, shift + even, across_0)
            stencils(source, even + 1, shift + even + 1, across_1)
            return carry

        lax.fori_loop(1, columns // 2, two_columns, 0)
        vertical(across_0, target, columns - 2, shift + columns - 2)
        vertical(across_1, target, columns - 1, shift + columns - 1)


def advect(steps, rows, staged_shape, places, parts, numbers, inverse):
    lanes = staged_shape[-1]
    wide = math.prod(staged_shape[:-2])
    length, computed = wide - 4 * steps, wide - 4
    anywhere = pl.BlockSpec(memory_space=pl.ANY)
    work = (length + 2 * steps) * steps * rows * lanes
    return pl.pallas_call(
        functools.partial(advect_kernel, steps, places),
        out_shape=jax.ShapeDtypeStruct((length, rows, lanes), jnp.bfloat16),
        in_specs=[anywhere] * (len(parts) + 2),
        out_specs=pl.BlockSpec(memory_space=pltpu.VMEM),
        scratch_shapes=[
            pltpu.VMEM(staged_shape, jnp.bfloat16),
            pltpu.VMEM((wide, rows, lanes), jnp.float32),
            pltpu.VMEM((wide, rows, lanes), jnp.float32),
            pltpu.VMEM((rows, lanes), jnp.bfloat16),
            pltpu.VMEM((rows, lanes), jnp.bfloat16),
            pltpu.VMEM(numbers.shape, jnp.float32),
            pltpu.VMEM((computed, 10, LEVELS + 8, lanes), jnp.float32),
            pltpu.VMEM(inverse.shape, jnp.bfloat16),
            pltpu.SemaphoreType.DMA((len(parts),)),
            pltpu.SemaphoreType.DMA,
            pltpu.SemaphoreType.DMA,
        ],
        compiler_params=pltpu.CompilerParams(vmem_limit_bytes=36 * 1024 * 1024),
        cost_estimate=pl.CostEstimate(flops=work * 30 * (2 * LEVELS + 20), bytes_accessed=numbers.size * 4, transcendentals=0),
    )(*parts, numbers, inverse)


def from_below(array, width):
    peers = lax.axis_size("tile")
    return lax.ppermute(array[array.shape[0] - width:], "tile", [(i, (i + 1) % peers) for i in range(peers)])


def from_above(array, width):
    peers = lax.axis_size("tile")
    return lax.ppermute(array[:width], "tile", [((i + 1) % peers, i) for i in range(peers)])


def twice(inverse):
    empty = jnp.zeros_like(inverse)
    return jnp.concatenate([jnp.concatenate([inverse, empty], 2), jnp.concatenate([empty, inverse], 2)], 1)


def shards(ensemble, weights, patch_index, courant, vert_inverse):
    peers = lax.axis_size("mem")
    members, levels, length, lanes = ensemble.shape
    share = length // peers
    rows = members * levels // GROUPS
    halo, shift = 4 * HALF, 2 * HALF
    below, above = shift - 2, halo - 2

    to_send = jnp.transpose(ensemble.reshape(members, levels, peers, share, lanes), (3, 2, 0, 1, 4))
    to_send = [to_send[part] for part in range(share)]
    arrived = [lax.all_to_all(to_send[0], "mem", split_axis=0, concat_axis=0, tiled=True)]

    patches = lax.dynamic_slice_in_dim(patch_index, lax.axis_index("mem") * share, share, 0)
    turned = lax.optimization_barrier(jnp.swapaxes(weights, 1, 2))
    chosen = jnp.take(turned, patches, axis=0, mode="clip")
    numbers = jnp.transpose(courant, (2, 0, 1, 3))
    tied, numbers_above, inverse_above, chosen = lax.optimization_barrier(
        (to_send[1], from_above(numbers, above), from_above(vert_inverse, above), chosen))
    arrived.append(lax.all_to_all(tied, "mem", split_axis=0, concat_axis=0, tiled=True))
    numbers_first = jnp.concatenate([numbers[2:], numbers_above])
    inverse_first = twice(jnp.concatenate([vert_inverse[2:], inverse_above]))

    returned, sides = [], []
    for part in range(share):
        blended = jnp.einsum("joc,clj->olj", chosen[part], arrived[part].reshape(-1, levels, lanes),
                             preferred_element_type=jnp.float32).astype(jnp.bfloat16)
        blended = blended.reshape(arrived[part].shape)
        back = lax.all_to_all(blended, "mem", split_axis=0, concat_axis=0, tiled=True)
        returned.append(back.reshape(peers, GROUPS, rows, lanes))
        sides.append([from_above(returned[part][:, group], halo // share) for group in range(GROUPS)])

    wide = (length + halo) // share
    fields = []
    for group in range(GROUPS):
        if group == 1:
            numbers_first, numbers_below, inverse_below = lax.optimization_barrier(
                (numbers_first, from_below(numbers, below), from_below(vert_inverse, below)))
        parts = returned + [sides[part][group] for part in range(share)]
        places = [(group, 0, part) for part in range(share)] + [(None, peers, part) for part in range(share)]
        fields.append(advect(HALF, rows, (wide, share, rows, lanes), places, parts, numbers_first, inverse_first))

    numbers_last = jnp.concatenate([numbers_below, numbers, numbers_above[:below]])
    inverse_last = twice(jnp.concatenate([inverse_below, vert_inverse, inverse_above[:below]]))
    places = [(None, 0, None), (None, halo, None)]
    fields = [advect(HALF, rows, (halo + length, rows, lanes), places, [from_below(field, halo), field],
                     numbers_last, inverse_last) for field in fields]
    forecast = jnp.stack(fields, axis=1).reshape(length, members, levels, lanes)
    return jnp.transpose(forecast, (1, 2, 0, 3))


def solution(mesh):
    return jax.shard_map(
        shards,
        mesh=mesh,
        in_specs=(
            P("mem", None, "tile", None),
            P("tile", None, None),
            P("tile", None),
            P(None, None, "tile", None),
            P("tile", None, None),
        ),
        out_specs=P("mem", None, "tile", None),
        check_vma=False,
    )
```

```python
import functools
import math

import jax
import jax.numpy as jnp
from jax import lax
from jax.experimental import pallas as pl
from jax.experimental.layout import Layout, with_layout_constraint
from jax.experimental.pallas import tpu as pltpu
from jax.sharding import PartitionSpec as P

HALF = 3
GROUPS = 2
LEVELS = 72
PAIR = 2 * LEVELS
TILE_ROWS = 16
LANES = 128


def stencil_weights(numbers):
    location = -jnp.abs(numbers)
    below, above, further = location - 1.0, location + 1.0, location + 2.0
    inner, outer = location * below, further * above
    far = above * inner * (-1.0 / 6.0)
    near = further * inner * 0.5
    mid = outer * below * -0.5
    ahead = outer * location * (1.0 / 6.0)
    forward = numbers >= 0.0
    return [
        jnp.where(forward, far, 0.0),
        jnp.where(forward, near, ahead),
        mid,
        jnp.where(forward, ahead, near),
        jnp.where(forward, 0.0, far),
    ]


def weighted(values, weights):
    total = values[0] * weights[0]
    for value, weight in zip(values[1:], weights[1:]):
        total = total + value * weight
    return total


def advect_kernel(steps, places, *refs):
    parts, (numbers, inverse, out), scratch = refs[:len(places)], refs[len(places):len(places) + 3], refs[len(places) + 3:]
    staged, field, other, across_0, across_1, number, weight, operator, field_sem, number_sem, operator_sem = scratch
    length, rows, _ = out.shape
    computed = length + 4 * (steps - 1)
    pairs = rows // PAIR
    loads = [
        pltpu.make_async_copy(numbers, number, number_sem),
        pltpu.make_async_copy(inverse, operator, operator_sem),
    ]
    for index, (ref, place) in enumerate(zip(parts, places)):
        group, start, offset = place
        source = ref if group is None else ref.at[:, group]
        target = staged.at[pl.ds(start, ref.shape[0]), offset] if offset is not None else staged.at[pl.ds(start, ref.shape[0])]
        loads.append(pltpu.make_async_copy(source, target, field_sem.at[index]))
    for load in loads:
        load.start()
    for load in loads:
        load.wait()

    lane = lax.broadcasted_iota(jnp.int32, (8, LANES), 1)
    last = LANES - 1
    inside = [lane >= 2, lane >= 1, None, lane <= last - 1, lane <= last - 2]

    def prepare(column):
        for level in range(0, LEVELS, 8):
            at = pl.ds(level, 8)
            lon = stencil_weights(number[column, 0, at, :])
            lat = stencil_weights(number[column, 1, at, :])
            lat = [w if keep is None else jnp.where(keep, w, 0.0) for keep, w in zip(inside, lat)]
            for k, w in enumerate(lon + lat):
                weight[column, k, at, :] = w
                if level == 0:
                    weight[column, k, pl.ds(LEVELS, 8), :] = w

    def widen(column):
        if len(staged.shape) == 4:
            held = staged[column // 2, column % 2]
        else:
            held = staged[column]
        field[column] = held.astype(jnp.float32)

    def stencils(source, column, w_column, across):
        def lat_part(at, along, w):
            near = along.astype(jnp.bfloat16)
            shifted = [pltpu.roll(near, turn, 1).astype(jnp.float32) if turn else along
                       for turn in (2, 1, 0, LANES - 1, LANES - 2)]
            across[at, :] = weighted(shifted, w).astype(jnp.bfloat16)

        for tile in range(PAIR // TILE_ROWS):
            level = (tile * TILE_ROWS) % LEVELS
            w = [weight[w_column, k, pl.ds(level, TILE_ROWS), :] for k in range(10)]
            for pair in range(pairs):
                at = pl.ds(pair * PAIR + tile * TILE_ROWS, TILE_ROWS)
                lat_part(at, weighted([source[column + k, at, :] for k in range(5)], w[:5]), w[5:])

    def vertical(across, target, column, w_column):
        side = jnp.concatenate([across[pl.ds(pair * PAIR, PAIR), :] for pair in range(pairs)], axis=1)
        mixed = jnp.dot(operator[w_column], side, preferred_element_type=jnp.float32).astype(jnp.bfloat16)
        for pair in range(pairs):
            target[column, pl.ds(pair * PAIR, PAIR), :] = mixed[:, pair * LANES:(pair + 1) * LANES].astype(target.dtype)

    buffers = (field, other)
    for step in range(steps):
        source = buffers[step % 2]
        target = out if step == steps - 1 else buffers[(step + 1) % 2]
        columns = length + 4 * (steps - 1 - step)
        shift = 2 * step

        def ready(column):
            if step == 0:
                widen(column + 4)
                prepare(column)

        if step == 0:
            for column in range(4):
                widen(column)
        ready(0)
        ready(1)
        stencils(source, 0, shift, across_0)
        stencils(source, 1, shift + 1, across_1)

        def two_columns(index, carry):
            even = 2 * index
            vertical(across_0, target, even - 2, shift + even - 2)
            vertical(across_1, target, even - 1, shift + even - 1)
            ready(even)
            ready(even + 1)
            stencils(source, even, shift + even, across_0)
            stencils(source, even + 1, shift + even + 1, across_1)
            return carry

        lax.fori_loop(1, columns // 2, two_columns, 0)
        vertical(across_0, target, columns - 2, shift + columns - 2)
        vertical(across_1, target, columns - 1, shift + columns - 1)


def advect(steps, rows, staged_shape, places, parts, numbers, inverse):
    lanes = staged_shape[-1]
    wide = math.prod(staged_shape[:-2])
    length, computed = wide - 4 * steps, wide - 4
    anywhere = pl.BlockSpec(memory_space=pl.ANY)
    work = (length + 2 * steps) * steps * rows * lanes
    return pl.pallas_call(
        functools.partial(advect_kernel, steps, places),
        out_shape=jax.ShapeDtypeStruct((length, rows, lanes), jnp.bfloat16),
        in_specs=[anywhere] * (len(parts) + 2),
        out_specs=pl.BlockSpec(memory_space=pltpu.VMEM),
        scratch_shapes=[
            pltpu.VMEM(staged_shape, jnp.bfloat16),
            pltpu.VMEM((wide, rows, lanes), jnp.float32),
            pltpu.VMEM((wide, rows, lanes), jnp.float32),
            pltpu.VMEM((rows, lanes), jnp.bfloat16),
            pltpu.VMEM((rows, lanes), jnp.bfloat16),
            pltpu.VMEM(numbers.shape, jnp.float32),
            pltpu.VMEM((computed, 10, LEVELS + 8, lanes), jnp.float32),
            pltpu.VMEM(inverse.shape, jnp.bfloat16),
            pltpu.SemaphoreType.DMA((len(parts),)),
            pltpu.SemaphoreType.DMA,
            pltpu.SemaphoreType.DMA,
        ],
        compiler_params=pltpu.CompilerParams(vmem_limit_bytes=36 * 1024 * 1024),
        cost_estimate=pl.CostEstimate(flops=work * 30 * (2 * LEVELS + 20), bytes_accessed=numbers.size * 4, transcendentals=0),
    )(*parts, numbers, inverse)


def from_below(array, width):
    peers = lax.axis_size("tile")
    return lax.ppermute(array[array.shape[0] - width:], "tile", [(i, (i + 1) % peers) for i in range(peers)])


def from_above(array, width):
    peers = lax.axis_size("tile")
    return lax.ppermute(array[:width], "tile", [((i + 1) % peers, i) for i in range(peers)])


def copied_from(step, array):
    peers, tiles = lax.axis_size("mem"), lax.axis_size("tile")
    pairs = []
    for mem in range(peers):
        for tile in range(tiles):
            source = (tile + step) % tiles
            holder = mem if source // 2 == tile // 2 else mem ^ 1
            pairs.append((holder * tiles + source, mem * tiles + tile))
    return lax.ppermute(array, ("mem", "tile"), pairs)


def twice(inverse):
    empty = jnp.zeros_like(inverse)
    return jnp.concatenate([jnp.concatenate([inverse, empty], 2), jnp.concatenate([empty, inverse], 2)], 1)


def shards(ensemble, weights, patch_index, courant, vert_inverse):
    peers = lax.axis_size("mem")
    members, levels, length, lanes = ensemble.shape
    share = length // peers
    rows = members * levels // GROUPS
    halo, shift = 4 * HALF, 2 * HALF
    below, above = shift - 2, halo - 2

    to_send = jnp.transpose(ensemble.reshape(members, levels, peers, share, lanes), (3, 2, 0, 1, 4))
    to_send = [to_send[part] for part in range(share)]
    arrived = [lax.all_to_all(to_send[0], "mem", split_axis=0, concat_axis=0, tiled=True)]

    patches = lax.dynamic_slice_in_dim(patch_index, lax.axis_index("mem") * share, share, 0)
    turned = lax.optimization_barrier(with_layout_constraint(jnp.swapaxes(weights, 1, 2), Layout((0, 1, 2))))
    chosen = jnp.take(turned, patches, axis=0, mode="clip")
    numbers = jnp.transpose(courant, (2, 0, 1, 3))
    narrow = numbers.astype(jnp.bfloat16)
    tied, numbers_above, inverse_above, chosen = lax.optimization_barrier(
        (to_send[1], copied_from(1, narrow[:above]), copied_from(1, vert_inverse[:above]), chosen))
    arrived.append(lax.all_to_all(tied, "mem", split_axis=0, concat_axis=0, tiled=True))
    numbers_above = numbers_above.astype(jnp.float32)

    returned = []
    for part in range(share):
        blended = jnp.einsum("joc,clj->olj", chosen[part], arrived[part].reshape(-1, levels, lanes),
                             preferred_element_type=jnp.float32).astype(jnp.bfloat16)
        blended = blended.reshape(arrived[part].shape)
        if part == share - 1:
            blended, numbers_below, inverse_below = lax.optimization_barrier(
                (blended, copied_from(-1, narrow[length - below:]), copied_from(-1, vert_inverse[length - below:])))
        back = lax.all_to_all(blended, "mem", split_axis=0, concat_axis=0, tiled=True)
        returned.append(back.reshape(peers, GROUPS, rows, lanes))
    numbers_below = numbers_below.astype(jnp.float32)

    near = halo // share
    sides = [from_above(jnp.stack([back[:near, group] for back in returned], axis=1), near) for group in range(GROUPS)]

    numbers_first = jnp.concatenate([numbers[2:], numbers_above])
    inverse_first = twice(jnp.concatenate([vert_inverse[2:], inverse_above]))
    wide = (length + halo) // share
    fields = []
    for group in range(GROUPS):
        parts = returned + [sides[group]]
        places = [(group, 0, 0), (group, 0, 1), (None, peers, None)]
        fields.append(advect(HALF, rows, (wide, share, rows, lanes), places, parts, numbers_first, inverse_first))

    numbers_last = jnp.concatenate([numbers_below, numbers, numbers_above[:below]])
    inverse_last = twice(jnp.concatenate([inverse_below, vert_inverse, inverse_above[:below]]))
    places = [(None, 0, None), (None, halo, None)]
    fields = [advect(HALF, rows, (halo + length, rows, lanes), places, [from_below(field, halo), field],
                     numbers_last, inverse_last) for field in fields]
    forecast = jnp.stack(fields, axis=1).reshape(length, members, levels, lanes)
    return jnp.transpose(forecast, (1, 2, 0, 3))


def solution(mesh):
    return jax.shard_map(
        shards,
        mesh=mesh,
        in_specs=(
            P("mem", None, "tile", None),
            P("tile", None, None),
            P("tile", None),
            P(None, None, "tile", None),
            P("tile", None, None),
        ),
        out_specs=P("mem", None, "tile", None),
        check_vma=False,
    )
```

```python
import functools
import math

import jax
import jax.numpy as jnp
from jax import lax
from jax.experimental import pallas as pl
from jax.experimental.layout import Layout, with_layout_constraint
from jax.experimental.pallas import tpu as pltpu
from jax.sharding import PartitionSpec as P

HALF = 3
GROUPS = 2
LEVELS = 72
PAIR = 2 * LEVELS
TILE_ROWS = 16
LANES = 128


def stencil_weights(numbers):
    location = -jnp.abs(numbers)
    below, above, further = location - 1.0, location + 1.0, location + 2.0
    inner, outer = location * below, further * above
    far = above * inner * (-1.0 / 6.0)
    near = further * inner * 0.5
    mid = outer * below * -0.5
    ahead = outer * location * (1.0 / 6.0)
    forward = numbers >= 0.0
    return [
        jnp.where(forward, far, 0.0),
        jnp.where(forward, near, ahead),
        mid,
        jnp.where(forward, ahead, near),
        jnp.where(forward, 0.0, far),
    ]


def weighted(values, weights):
    total = values[0] * weights[0]
    for value, weight in zip(values[1:], weights[1:]):
        total = total + value * weight
    return total


def advect_kernel(steps, places, numbers_at, mode, *refs):
    outs = 1 if mode != "inner" else steps
    parts, refs = refs[:len(places)], refs[len(places):]
    borders, refs = (refs[:steps], refs[steps:]) if mode == "outer" else ((), refs)
    (numbers, inverse, out), refs = refs[:3], refs[3:]
    edges, scratch = refs[:outs - 1], refs[outs - 1:]
    staged, border, field, other, across_0, across_1, number, weight, operator, field_sem, border_sem, number_sem, operator_sem = scratch
    rows = out.shape[1]
    computed, wide = number.shape[0], field.shape[0]
    pairs = rows // PAIR
    matrices = pltpu.make_async_copy(inverse.at[pl.ds(numbers_at, computed)], operator, operator_sem)
    loads = [pltpu.make_async_copy(numbers.at[pl.ds(numbers_at, computed)], number, number_sem)]
    for index, (ref, place) in enumerate(zip(parts, places)):
        group, begin, count, start, offset = place
        source = ref.at[pl.ds(begin, count)] if group is None else ref.at[pl.ds(begin, count), group]
        target = staged.at[pl.ds(start, count)] if offset is None else staged.at[pl.ds(start, count), offset]
        loads.append(pltpu.make_async_copy(source, target, field_sem.at[index]))
    for index, ref in enumerate(borders):
        loads.append(pltpu.make_async_copy(ref, border.at[index], border_sem.at[index]))
    for load in loads:
        load.start()
    matrices.start()
    for load in loads:
        load.wait()

    lane = lax.broadcasted_iota(jnp.int32, (8, LANES), 1)
    last = LANES - 1
    inside = [lane >= 2, lane >= 1, None, lane <= last - 1, lane <= last - 2]

    def prepare(column):
        for level in range(0, LEVELS, 8):
            at = pl.ds(level, 8)
            lon = stencil_weights(number[column, 0, at, :])
            lat = stencil_weights(number[column, 1, at, :])
            lat = [w if keep is None else jnp.where(keep, w, 0.0) for keep, w in zip(inside, lat)]
            for k, w in enumerate(lon + lat):
                weight[column, k, at, :] = w
                if level == 0:
                    weight[column, k, pl.ds(LEVELS, 8), :] = w

    def widen(column):
        if len(staged.shape) == 4:
            held = staged[column // 2, column % 2]
        else:
            held = staged[column]
        field[column] = held.astype(jnp.float32)

    def stencils(source, column, w_column, across):
        def lat_part(at, along, w):
            near = along.astype(jnp.bfloat16)
            shifted = [pltpu.roll(near, turn, 1).astype(jnp.float32) if turn else along
                       for turn in (2, 1, 0, LANES - 1, LANES - 2)]
            across[at, :] = weighted(shifted, w).astype(jnp.bfloat16)

        for tile in range(PAIR // TILE_ROWS):
            level = (tile * TILE_ROWS) % LEVELS
            w = [weight[w_column, k, pl.ds(level, TILE_ROWS), :] for k in range(10)]
            for pair in range(pairs):
                at = pl.ds(pair * PAIR + tile * TILE_ROWS, TILE_ROWS)
                lat_part(at, weighted([source[column + k, at, :] for k in range(5)], w[:5]), w[5:])

    def vertical(across, target, column, w_column):
        side = jnp.concatenate([across[pl.ds(pair * PAIR, PAIR), :] for pair in range(pairs)], axis=1)
        mixed = jnp.dot(operator[w_column], side, preferred_element_type=jnp.float32).astype(jnp.bfloat16)
        for pair in range(pairs):
            target[column + lead, pl.ds(pair * PAIR, PAIR), :] = mixed[:, pair * LANES:(pair + 1) * LANES].astype(target.dtype)

    buffers = (field, other)
    lead = 4 if mode == "outer" else 0
    for column in range(2 * steps - 2 if lead else 0):
        prepare(column)
    for step in range(steps):
        source = buffers[step % 2]
        target = out if step == steps - 1 else buffers[(step + 1) % 2]
        columns = wide - 4 if lead else wide - 4 * (step + 1)
        shift = 2 * (steps - 1 - step) if lead else 2 * step
        if lead:
            target[pl.ds(0, lead)] = border[step].astype(target.dtype)

        def ready(column):
            if step == 0:
                widen(column + 4)
                prepare(column + shift)

        if step == 0:
            for column in range(4):
                widen(column)
        ready(0)
        ready(1)
        stencils(source, 0, shift, across_0)
        stencils(source, 1, shift + 1, across_1)
        if step == 0:
            matrices.wait()

        def two_columns(index, carry):
            even = 2 * index
            vertical(across_0, target, even - 2, shift + even - 2)
            vertical(across_1, target, even - 1, shift + even - 1)
            ready(even)
            ready(even + 1)
            stencils(source, even, shift + even, across_0)
            stencils(source, even + 1, shift + even + 1, across_1)
            return carry

        lax.fori_loop(1, columns // 2, two_columns, 0)
        vertical(across_0, target, columns - 2, shift + columns - 2)
        vertical(across_1, target, columns - 1, shift + columns - 1)
        if mode == "inner" and step < steps - 1:
            edges[step][...] = target[pl.ds(columns - 4, 4)].astype(jnp.bfloat16)


def advect(steps, rows, staged_shape, places, parts, numbers, inverse, numbers_at=0, mode="whole", borders=()):
    lanes = staged_shape[-1]
    wide = math.prod(staged_shape[:-2])
    outer = mode == "outer"
    length = wide if outer else wide - 4 * steps
    computed = wide - 4 + (2 * steps - 2 if outer else 0)
    anywhere = pl.BlockSpec(memory_space=pl.ANY)
    work = (wide - 2 * steps) * steps * rows * lanes
    out = jax.ShapeDtypeStruct((length, rows, lanes), jnp.bfloat16)
    outs = [out] * (steps if mode == "inner" else 1)
    given = pl.pallas_call(
        functools.partial(advect_kernel, steps, places, numbers_at, mode),
        out_shape=outs,
        in_specs=[anywhere] * (len(parts) + len(borders) + 2),
        out_specs=[pl.BlockSpec(memory_space=pltpu.VMEM)] * len(outs),
        scratch_shapes=[
            pltpu.VMEM(staged_shape, jnp.bfloat16),
            pltpu.VMEM((steps, 4, rows, lanes) if outer else (1, 1, 16, lanes), jnp.bfloat16),
            pltpu.VMEM((wide, rows, lanes), jnp.float32),
            pltpu.VMEM((wide, rows, lanes), jnp.float32),
            pltpu.VMEM((rows, lanes), jnp.bfloat16),
            pltpu.VMEM((rows, lanes), jnp.bfloat16),
            pltpu.VMEM((computed,) + numbers.shape[1:], jnp.float32),
            pltpu.VMEM((computed, 10, LEVELS + 8, lanes), jnp.float32),
            pltpu.VMEM((computed,) + inverse.shape[1:], jnp.bfloat16),
            pltpu.SemaphoreType.DMA((len(parts),)),
            pltpu.SemaphoreType.DMA((max(1, len(borders)),)),
            pltpu.SemaphoreType.DMA,
            pltpu.SemaphoreType.DMA,
        ],
        compiler_params=pltpu.CompilerParams(vmem_limit_bytes=36 * 1024 * 1024),
        cost_estimate=pl.CostEstimate(flops=work * 30 * (2 * LEVELS + 20), bytes_accessed=numbers.size * 4, transcendentals=0),
    )(*parts, *borders, numbers, inverse)
    return given if mode == "inner" else given[0]


def from_below(array, width):
    peers = lax.axis_size("tile")
    return lax.ppermute(array[array.shape[0] - width:], "tile", [(i, (i + 1) % peers) for i in range(peers)])


def from_above(array, width):
    peers = lax.axis_size("tile")
    return lax.ppermute(array[:width], "tile", [((i + 1) % peers, i) for i in range(peers)])


def copied_from(step, array):
    peers, tiles = lax.axis_size("mem"), lax.axis_size("tile")
    pairs = []
    for mem in range(peers):
        for tile in range(tiles):
            source = (tile + step) % tiles
            holder = mem if source // 2 == tile // 2 else mem ^ 1
            pairs.append((holder * tiles + source, mem * tiles + tile))
    return lax.ppermute(array, ("mem", "tile"), pairs)


def twice(inverse):
    empty = jnp.zeros_like(inverse)
    return jnp.concatenate([jnp.concatenate([inverse, empty], 2), jnp.concatenate([empty, inverse], 2)], 1)


def shards(ensemble, weights, patch_index, courant, vert_inverse):
    peers = lax.axis_size("mem")
    members, levels, length, lanes = ensemble.shape
    share = length // peers
    rows = members * levels // GROUPS
    halo, shift = 4 * HALF, 2 * HALF
    below, above = shift - 2, halo - 2

    to_send = jnp.transpose(ensemble.reshape(members, levels, peers, share, lanes), (3, 2, 0, 1, 4))
    to_send = [to_send[part] for part in range(share)]
    arrived = [lax.all_to_all(to_send[0], "mem", split_axis=0, concat_axis=0, tiled=True)]

    patches = lax.dynamic_slice_in_dim(patch_index, lax.axis_index("mem") * share, share, 0)
    turned = lax.optimization_barrier(with_layout_constraint(jnp.swapaxes(weights, 1, 2), Layout((0, 1, 2))))
    chosen = jnp.take(turned, patches, axis=0, mode="clip")
    numbers = jnp.transpose(courant, (2, 0, 1, 3))
    narrow = numbers.astype(jnp.bfloat16)
    tied, numbers_above, inverse_above, chosen = lax.optimization_barrier(
        (to_send[1], copied_from(1, narrow[:above]), copied_from(1, vert_inverse[:above]), chosen))
    arrived.append(lax.all_to_all(tied, "mem", split_axis=0, concat_axis=0, tiled=True))
    numbers_above = numbers_above.astype(jnp.float32)

    returned = []
    for part in range(share):
        blended = jnp.einsum("joc,clj->olj", chosen[part], arrived[part].reshape(-1, levels, lanes),
                             preferred_element_type=jnp.float32).astype(jnp.bfloat16)
        blended = blended.reshape(arrived[part].shape)
        if part == share - 1:
            blended, numbers_below, inverse_below = lax.optimization_barrier(
                (blended, copied_from(-1, narrow[length - below:]), copied_from(-1, vert_inverse[length - below:])))
        back = lax.all_to_all(blended, "mem", split_axis=0, concat_axis=0, tiled=True)
        returned.append(back.reshape(peers, GROUPS, rows, lanes))
    numbers_below = numbers_below.astype(jnp.float32)

    near = halo // share
    sides = [from_above(jnp.stack([back[:near, group] for back in returned], axis=1), near) for group in range(GROUPS)]

    numbers_first = jnp.concatenate([numbers[2:], numbers_above])
    inverse_first = twice(jnp.concatenate([vert_inverse[2:], inverse_above]))
    fields = []
    for group in range(GROUPS):
        places = [(group, 0, peers, 0, part) for part in range(share)]
        inner = advect(HALF, rows, (peers, share, rows, lanes), places, returned, numbers_first, inverse_first, 0, "inner")
        places = [(group, peers - 2, 2, 0, part) for part in range(share)] + [(None, 0, near, 2, None)]
        fields.append(advect(HALF, rows, (near + 2, share, rows, lanes), places, returned + [sides[group]],
                             numbers_first, inverse_first, 2 * HALF + 2, "outer", inner[1:] + inner[:1]))

    numbers_last = jnp.concatenate([numbers_below, numbers, numbers_above[:below]])
    inverse_last = twice(jnp.concatenate([inverse_below, vert_inverse, inverse_above[:below]]))
    places = [(None, 0, halo, 0, None), (None, 0, length, halo, None)]
    fields = [advect(HALF, rows, (halo + length, rows, lanes), places, [from_below(field, halo), field],
                     numbers_last, inverse_last) for field in fields]
    forecast = jnp.stack(fields, axis=1).reshape(length, members, levels, lanes)
    return jnp.transpose(forecast, (1, 2, 0, 3))


def solution(mesh):
    return jax.shard_map(
        shards,
        mesh=mesh,
        in_specs=(
            P("mem", None, "tile", None),
            P("tile", None, None),
            P("tile", None),
            P(None, None, "tile", None),
            P("tile", None, None),
        ),
        out_specs=P("mem", None, "tile", None),
        check_vma=False,
    )
```
